32 devices in a mesh: chan: 4 (over z), seg: 4 (over x, core), lag: 2 (over y).
Axes of the slice: x: 2, y: 2, z: 4, core: 2. Of those that a mesh axis runs over, the one named last changes fastest.
Arguments:
- spectra: bfloat16 [4, 2500, 2, 6144], P('seg', 'chan', None, 'lag'), may hold values from -6 to 6
- pair_local: int32 [4, 3, 256], replicated, may hold values from 0 to 624
- pair_partner: int32 [4, 3, 256], replicated, may hold values from 0 to 624, as said below
- pair_bin: int32 [4, 3, 256], replicated, may hold values from 0 to 1
- pair_owner: int32 [4, 3, 256], replicated, may hold values 0 or 1
- pair_count: int32 [4, 3], replicated, may hold values from 64 to 256, as said below
Outputs:
- stacks: float32 [2500, 2, 2048], P('chan', None, 'lag')
The draws below stay inside these ranges and needn't reach their ends.
Inputs may be any that keep to these rules, and one draw needn't show every extreme that they name: `pair_partner`: in round 0 the two channels of a pair differ. `pair_count`: some block reaches 256 in some round.
All inputs are finite; a program needn't handle non-finite values.
Results may differ from the reference program's by a relative error of at most 0.0065.
Values may be sent and summed in bfloat16 or wider, within the bound.
A program may use at most 128 MiB of HBM per device.

```python
import math
import jax
import jax.numpy as jnp
from jax import lax

FREQ = 6144
LAGS = 2048
CB = 625
PAIRS = 256
ROUNDS = 3
BINS = 2
SEGS = 4
BLOCKS = 4
CHANNELS = 2500


def pair_fields(key):
    base_key = jax.random.fold_in(key, 7)
    local_ids = jax.random.randint(jax.random.fold_in(base_key, 1), (BLOCKS, ROUNDS, PAIRS), 0, CB)
    step_ids = jax.random.randint(jax.random.fold_in(base_key, 2), (BLOCKS, ROUNDS, PAIRS), 1, CB)
    return (local_ids.astype(jnp.int32), jnp.mod(local_ids + step_ids, CB).astype(jnp.int32))


def draw_pair_local(key, part):
    return pair_fields(key)[0]


def draw_pair_partner(key, part):
    return pair_fields(key)[1]


def draw_pair_count(key, part):
    counts = jax.random.randint(jax.random.fold_in(key, 11), (BLOCKS * ROUNDS,), max(PAIRS // 4, 1), PAIRS + 1)
    chosen = jax.random.randint(jax.random.fold_in(key, 13), (), 0, BLOCKS * ROUNDS)
    counts = jnp.where(jnp.arange(BLOCKS * ROUNDS, dtype=jnp.int32) == chosen, PAIRS, counts)
    return counts.reshape(BLOCKS, ROUNDS).astype(jnp.int32)


def plant(entries, key, low, high):
    shape = entries.shape
    place = [jax.random.randint(jax.random.fold_in(key, axis), (), 0, shape[axis]) for axis in range(len(shape))]
    entries = entries.at[tuple(place)].set(low)
    longest = shape.index(max(shape))
    place[longest] = (place[longest] + 1) % shape[longest]
    return entries.at[tuple(place)].set(high)


def block_scale(rng, extent, pieces, low, largest):
    level = 1.0
    for axis_at, blocks in pieces:
        heights = jax.random.uniform(jax.random.fold_in(jax.random.fold_in(rng, 6), axis_at), (blocks,), jnp.float32, low / len(pieces), largest / len(pieces))
        level = level * jnp.repeat(jnp.exp(heights), extent[axis_at] // blocks).reshape((-1,) + (1,) * (len(extent) - 1 - axis_at))
    return level


def gaussian(own_key, dims, spread, bound, pieces=(), held_as=jnp.bfloat16):
    result = spread * jax.random.normal(own_key, dims, jnp.float32)
    if pieces:
        result = result * block_scale(own_key, dims, pieces, -0.22, 0.18)
    return jnp.clip(result, -bound, bound).astype(held_as)


def setup_inputs(seed: int = 0) -> dict:
    keys = jax.random.split(jax.random.key(seed), 7)
    return {
        "spectra": gaussian(keys[0], (SEGS, CHANNELS, 2, FREQ), 0.7, 6.0, ((0, 4), (1, 4), (3, 2))),
        "pair_local": draw_pair_local(jax.random.fold_in(keys[6], 71), 0),
        "pair_partner": draw_pair_partner(jax.random.fold_in(keys[6], 71), 0),
        "pair_bin": plant(jax.random.randint(keys[3], (BLOCKS, ROUNDS, PAIRS), 0, BINS), jax.random.fold_in(keys[3], 1), 0, BINS - 1).astype(jnp.int32),
        "pair_owner": plant((jax.random.randint(keys[4], (BLOCKS, ROUNDS, PAIRS), 0, 2) < 1).astype(jnp.int32), jax.random.fold_in(keys[4], 1), 0, 1),
        "pair_count": draw_pair_count(jax.random.fold_in(keys[6], 71), 0),
    }


def table_rows(taus):
    freq_index = jnp.arange(FREQ, dtype=jnp.int32) + 1
    phase = jnp.mod(taus[:, None] * freq_index[None, :], 2 * FREQ)
    angle = phase.astype(jnp.float32) * (math.pi / FREQ)
    return jnp.concatenate([jnp.cos(angle), -jnp.sin(angle)], axis=1).astype(jnp.bfloat16)


def reference(spectra, pair_local, pair_partner, pair_bin, pair_owner, pair_count):
    taus = jnp.arange(LAGS, dtype=jnp.int32) - LAGS // 2
    table = table_rows(taus).astype(jnp.float32)
    corr_scale = FREQ ** -0.5
    blocks = spectra.reshape(SEGS, BLOCKS, CB, 2, FREQ)
    stacks = jnp.zeros((CHANNELS * BINS, LAGS), jnp.float32)
    for round_index in range(ROUNDS):
        def one_block(block_index):
            partner_index = jnp.mod(block_index + round_index, BLOCKS)
            first = jnp.take(blocks, block_index, axis=1)
            second = jnp.take(blocks, partner_index, axis=1)
            first = jnp.take(first, pair_local[block_index, round_index], axis=1).astype(jnp.float32)
            second = jnp.take(second, pair_partner[block_index, round_index], axis=1).astype(jnp.float32)
            cross_real = first[:, :, 0] * second[:, :, 0] + first[:, :, 1] * second[:, :, 1]
            cross_imag = first[:, :, 1] * second[:, :, 0] - first[:, :, 0] * second[:, :, 1]
            cross = jnp.concatenate([cross_real, cross_imag], axis=2).astype(jnp.bfloat16).astype(jnp.float32)
            corr = jnp.einsum("spf,tf->spt", cross, table) * corr_scale
            return jnp.sum(corr, axis=0)
        corr_all = lax.map(one_block, jnp.arange(BLOCKS, dtype=jnp.int32))
        block_ids = jnp.arange(BLOCKS, dtype=jnp.int32)[:, None]
        partner_ids = jnp.mod(block_ids + round_index, BLOCKS)
        first_chan = block_ids * CB + pair_local[:, round_index]
        second_chan = partner_ids * CB + pair_partner[:, round_index]
        target = jnp.where(pair_owner[:, round_index] == 0, first_chan, second_chan)
        target_rows = (target * BINS + pair_bin[:, round_index]).reshape(-1)
        live = (jnp.arange(PAIRS, dtype=jnp.int32)[None, :] < pair_count[:, round_index][:, None]).astype(jnp.float32)
        weighted = (corr_all * live[:, :, None]).reshape(BLOCKS * PAIRS, LAGS)
        stacks = stacks.at[target_rows].add(weighted)
    return stacks.reshape(CHANNELS, BINS, LAGS)
```

```python
import math

import jax
import jax.numpy as jnp
from jax import lax
from jax.sharding import PartitionSpec as P

FREQ = 6144
LAGS = 2048
ROUNDS = 3
BINS = 2
FINE = 32
BF16 = jnp.bfloat16


def shifted(block, axis, distance):
    devices = range(lax.axis_size(axis))
    route = [((i - distance) % len(devices), i) for i in devices]
    return lax.ppermute(block, axis, route)


def contract_last(a, b, out_type=jnp.float32):
    return lax.dot_general(a, b, (((1,), (1,)), ((), ())), preferred_element_type=out_type)


def pick_rows(planes, index):
    ids = jnp.arange(planes.shape[0], dtype=jnp.int32)
    hot = (index[:, None] == ids[None, :]).astype(BF16)
    return lax.dot_general(hot, planes, (((1,), (0,)), ((), ())), preferred_element_type=BF16)


def cross_spectra(first, second):
    half = first.shape[1] // 2
    a, b = first.astype(jnp.float32), second.astype(jnp.float32)
    ar, ai, br, bi = a[:, :half], a[:, half:], b[:, :half], b[:, half:]
    return jnp.concatenate([ar * br + ai * bi, ai * br - ar * bi], axis=1).astype(BF16)


def make_table(freq_index):
    def small(taus):
        phase = jnp.mod(taus[:, None] * freq_index[None, :], 2 * FREQ)
        angle = phase.astype(jnp.float32) * (math.pi / FREQ)
        return jnp.cos(angle), jnp.sin(angle)

    coarse = small(jnp.arange(LAGS // FINE, dtype=jnp.int32) * FINE - LAGS // 2)
    fine = small(jnp.arange(FINE, dtype=jnp.int32))
    (ca, sa), (cb, sb) = lax.optimization_barrier((coarse, fine))
    ca, sa, cb, sb = ca[:, None], sa[:, None], cb[None], sb[None]
    cos = (ca * cb - sa * sb).astype(BF16).reshape(LAGS, -1)
    neg_sin = (-(sa * cb + ca * sb)).astype(BF16).reshape(LAGS, -1)
    return jnp.concatenate([cos, neg_sin], axis=1)


def selector(rows, active, total_rows):
    ids = jnp.arange(total_rows, dtype=jnp.int32)[:, None]
    return ((ids == rows[None, :]) & active[None, :]).astype(BF16)


def per_device(spectra, pair_local, pair_partner, pair_bin, pair_owner, pair_count):
    blocks = lax.axis_size("chan")
    me = lax.axis_index("chan")
    lag_index = lax.axis_index("lag")
    own = spectra[0]
    block_chans, _, half_freq = own.shape
    half_lags = LAGS // lax.axis_size("lag")
    total_rows = block_chans * BINS
    slots = pair_local.shape[2]
    half = slots // 2
    slot_ids = jnp.arange(slots, dtype=jnp.int32)
    planes = jnp.concatenate([own[:, 0], own[:, 1]], axis=1)

    sent = {}
    for r in range(1, ROUNDS):
        before = lax.rem(me - r + blocks, blocks)
        to_first = pick_rows(planes, pair_partner[before, r, 0::2])
        to_partner = pick_rows(planes, pair_local[me, r, 1::2])
        cuts = [(0, half)] if r == 1 else [(0, half // 2), (half // 2, half)]
        for lo, hi in cuts:
            sent[r, lo, hi] = (
                shifted(to_first[lo:hi], "chan", -r),
                shifted(to_partner[lo:hi], "chan", r),
            )

    freq_index = lag_index * half_freq + jnp.arange(half_freq, dtype=jnp.int32) + 1
    table = make_table(freq_index)
    corr_scale = FREQ ** (-0.5)

    def correlate(cross):
        part = (contract_last(table, cross) * corr_scale).astype(BF16)
        return lax.psum_scatter(part, ("lag", "seg"), scatter_dimension=0, tiled=True)

    def chosen(b, r, step, lo, hi, owner):
        def cut(values):
            return values[step::2][lo:hi]

        channel = pair_local if owner == 0 else pair_partner
        rows = cut(channel[b, r]) * BINS + cut(pair_bin[b, r])
        live = cut(slot_ids) < pair_count[b, r]
        return rows, live & (cut(pair_owner[b, r]) == owner)

    pieces = []
    own_pairs = cross_spectra(
        pick_rows(planes, pair_local[me, 0]), pick_rows(planes, pair_partner[me, 0])
    )
    rows0 = jnp.where(pair_owner[me, 0] == 0, pair_local[me, 0], pair_partner[me, 0])
    pieces.append(
        (correlate(own_pairs), [(rows0 * BINS + pair_bin[me, 0], slot_ids < pair_count[me, 0])])
    )
    for (r, lo, hi), (second, first) in sent.items():
        before = lax.rem(me - r + blocks, blocks)
        here = hi - lo
        crosses = jnp.concatenate(
            [
                cross_spectra(pick_rows(planes, pair_local[me, r, 0::2][lo:hi]), second),
                cross_spectra(first, pick_rows(planes, pair_partner[before, r, 1::2][lo:hi])),
            ],
            axis=0,
        )
        corr = correlate(crosses)
        from_after = shifted(corr[:, here:], "chan", -r)
        from_before = shifted(corr[:, :here], "chan", r)
        pieces.append(
            (
                jnp.concatenate([corr, from_after, from_before], axis=1),
                [
                    chosen(me, r, 0, lo, hi, 0),
                    chosen(before, r, 1, lo, hi, 1),
                    chosen(me, r, 1, lo, hi, 0),
                    chosen(before, r, 0, lo, hi, 1),
                ],
            )
        )

    def stacked(some):
        corr = jnp.concatenate([piece for piece, _ in some], axis=1)
        corr = lax.all_gather(corr, "seg", axis=0, tiled=True)
        rows = jnp.concatenate([rows for _, picks in some for rows, _ in picks])
        active = jnp.concatenate([live for _, picks in some for _, live in picks])
        return contract_last(selector(rows, active, total_rows), corr)

    result = stacked(pieces[:-1]) + stacked(pieces[-1:])
    return result.reshape(block_chans, BINS, half_lags)


def solution(mesh):
    return jax.shard_map(
        per_device,
        mesh=mesh,
        in_specs=(P("seg", "chan", None, "lag"), P(), P(), P(), P(), P()),
        out_specs=P("chan", None, "lag"),
        check_vma=False,
    )
```

```python
import math

import jax
import jax.numpy as jnp
from jax import lax
from jax.experimental import pallas as pl
from jax.experimental.pallas import tpu as pltpu
from jax.sharding import PartitionSpec as P

FREQ = 6144
LAGS = 2048
ROUNDS = 3
BINS = 2
FINE = 32
BF16 = jnp.bfloat16


def shifted(block, axis, distance):
    devices = range(lax.axis_size(axis))
    route = [((i - distance) % len(devices), i) for i in devices]
    return lax.ppermute(block, axis, route)


def contract_last(a, b, out_type=jnp.float32):
    return lax.dot_general(a, b, (((1,), (1,)), ((), ())), preferred_element_type=out_type)


def pick_rows(planes, index):
    ids = jnp.arange(planes.shape[0], dtype=jnp.int32)
    hot = (index[:, None] == ids[None, :]).astype(BF16)
    return lax.dot_general(hot, planes, (((1,), (0,)), ((), ())), preferred_element_type=BF16)


def parts_of(rows):
    rows = rows.astype(jnp.float32)
    if rows.ndim == 3:
        return rows[:, 0], rows[:, 1]
    half = rows.shape[1] // 2
    return rows[:, :half], rows[:, half:]


def cross_spectra(first, second):
    ar, ai = parts_of(first)
    br, bi = parts_of(second)
    return jnp.concatenate([ar * br + ai * bi, ai * br - ar * bi], axis=1).astype(BF16)


def make_table(freq_index):
    def small(taus):
        phase = jnp.mod(taus[:, None] * freq_index[None, :], 2 * FREQ)
        angle = phase.astype(jnp.float32) * (math.pi / FREQ)
        return jnp.cos(angle), jnp.sin(angle)

    coarse = small(jnp.arange(LAGS // FINE, dtype=jnp.int32) * FINE - LAGS // 2)
    fine = small(jnp.arange(FINE, dtype=jnp.int32))
    (ca, sa), (cb, sb) = lax.optimization_barrier((coarse, fine))
    ca, sa, cb, sb = ca[:, None], sa[:, None], cb[None], sb[None]
    cos = (ca * cb - sa * sb).astype(BF16).reshape(LAGS, -1)
    neg_sin = (-(sa * cb + ca * sb)).astype(BF16).reshape(LAGS, -1)
    return jnp.concatenate([cos, neg_sin], axis=1)


def exchanged(axes, distance, block):
    route = [(i, i ^ distance) for i in range(math.prod(lax.axis_size(a) for a in axes))]
    return lax.ppermute(block, axes, route)


def summed(terms):
    total = terms[0].astype(jnp.float32)
    for term in terms[1:]:
        total = total + term.astype(jnp.float32)
    return total.astype(BF16)


def stack_kernel(rows_ref, corr_ref, out_ref):
    chans, bins, _ = out_ref.shape
    first = pl.program_id(0) * chans
    ids = first + lax.broadcasted_iota(jnp.int32, (chans, 1), 0)
    for k in range(bins):
        hot = jnp.where(ids * bins + k == rows_ref[...], 1.0, 0.0).astype(BF16)
        out_ref[:, k, :] = contract_last(hot, corr_ref[...])


def stack_rows(rows, corr, block_chans):
    lags, count = corr.shape
    tile = 128
    return pl.pallas_call(
        stack_kernel,
        grid=(pl.cdiv(block_chans, tile),),
        out_shape=jax.ShapeDtypeStruct((block_chans, BINS, lags), jnp.float32),
        in_specs=[
            pl.BlockSpec((1, count), lambda i: (0, 0)),
            pl.BlockSpec((lags, count), lambda i: (0, 0)),
        ],
        out_specs=pl.BlockSpec((tile, BINS, lags), lambda i: (i, 0, 0)),
        compiler_params=pltpu.CompilerParams(vmem_limit_bytes=40 * 2**20),
        cost_estimate=pl.CostEstimate(
            flops=2 * block_chans * BINS * lags * count,
            bytes_accessed=4 * block_chans * BINS * lags + 2 * lags * count,
            transcendentals=0,
        ),
    )(rows[None, :], corr)


def per_device(spectra, pair_local, pair_partner, pair_bin, pair_owner, pair_count):
    blocks = lax.axis_size("chan")
    segs, halves = lax.axis_size("seg"), lax.axis_size("lag")
    me = lax.axis_index("chan")
    lag_index = lax.axis_index("lag")
    seg_index = lax.axis_index("seg")
    own = spectra[0]
    block_chans, _, half_freq = own.shape
    half_lags = LAGS // halves
    share = half_lags // segs
    slots = pair_local.shape[2]
    half = slots // 2
    slot_ids = jnp.arange(slots, dtype=jnp.int32)

    def before(r):
        return lax.rem(me - r + blocks, blocks)

    def leaving(r, lo, hi):
        return pair_partner[before(r), r, 0::2][lo:hi], pair_local[me, r, 1::2][lo:hi]

    def arrive(r, to_first, to_partner):
        return shifted(to_first, "chan", -r), shifted(to_partner, "chan", r)

    near = arrive(1, *(jnp.take(own, index, axis=0) for index in leaving(1, 0, half)))
    planes = jnp.concatenate([own[:, 0], own[:, 1]], axis=1)
    far = arrive(2, *(pick_rows(planes, index) for index in leaving(2, 0, half)))

    freq_index = lag_index * half_freq + jnp.arange(half_freq, dtype=jnp.int32) + 1
    table = make_table(freq_index)
    corr_scale = FREQ ** (-0.5)

    def correlate(cross):
        return (contract_last(table, cross) * corr_scale).astype(BF16)

    def peers():
        for distance in range(1, halves * segs):
            lag, seg = lag_index ^ (distance % halves), seg_index ^ (distance // halves)
            yield distance, lag, seg

    def reduce_share(part):
        def cut(lag, seg):
            return lax.dynamic_slice_in_dim(part, lag * half_lags + seg * share, share, 0)

        terms = [cut(lag_index, seg_index)]
        for distance, lag, seg in peers():
            terms.append(exchanged(("seg", "lag"), distance, cut(lag, seg)))
        return summed(terms)

    def gather_shares(shares):
        whole = jnp.zeros((half_lags, shares.shape[1]), BF16)
        for distance in range(segs):
            block = exchanged(("seg",), distance, shares) if distance else shares
            whole = lax.dynamic_update_slice(whole, block, ((seg_index ^ distance) * share, 0))
        return whole

    def crosses(r, lo, hi, second, first):
        return [
            cross_spectra(pick_rows(planes, pair_local[me, r, 0::2][lo:hi]), second),
            cross_spectra(first, pick_rows(planes, pair_partner[before(r), r, 1::2][lo:hi])),
        ]

    def swapped(r, corr):
        here = corr.shape[1] // 2
        return [corr, shifted(corr[:, here:], "chan", -r), shifted(corr[:, :here], "chan", r)]

    def target(channel, b, r, owner, pick):
        live = (slot_ids < pair_count[b, r]) & (pair_owner[b, r] == owner)
        return pick(jnp.where(live, channel[b, r] * BINS + pair_bin[b, r], -1))

    def targets(r, lo, hi):
        even, odd = (lambda v: v[0::2][lo:hi]), (lambda v: v[1::2][lo:hi])
        return [
            target(pair_local, me, r, 0, even),
            target(pair_partner, before(r), r, 1, odd),
            target(pair_local, me, r, 0, odd),
            target(pair_partner, before(r), r, 1, even),
        ]

    own_cross = cross_spectra(
        pick_rows(planes, pair_local[me, 0]), pick_rows(planes, pair_partner[me, 0])
    )
    own_rows = jnp.where(pair_owner[me, 0] == 0, pair_local[me, 0], pair_partner[me, 0])
    own_rows = jnp.where(slot_ids < pair_count[me, 0], own_rows * BINS + pair_bin[me, 0], -1)

    near_part = correlate(jnp.concatenate([own_cross, *crosses(1, 0, half, *near)], axis=0))
    near_corr = reduce_share(near_part)
    near_pieces = [near_corr[:, :slots], *swapped(1, near_corr[:, slots:])]
    near_corr = gather_shares(jnp.concatenate(near_pieces, axis=1))
    near_corr, far = lax.optimization_barrier((near_corr, far))
    far_corr = reduce_share(correlate(jnp.concatenate(crosses(2, 0, half, *far), axis=0)))
    far_corr = gather_shares(jnp.concatenate(swapped(2, far_corr), axis=1))

    rows = [own_rows, *targets(1, 0, half), *targets(2, 0, half)]
    corr = jnp.concatenate([near_corr, far_corr], axis=1)
    return stack_rows(jnp.concatenate(rows), corr, block_chans)


def solution(mesh):
    return jax.shard_map(
        per_device,
        mesh=mesh,
        in_specs=(P("seg", "chan", None, "lag"), P(), P(), P(), P(), P()),
        out_specs=P("chan", None, "lag"),
        check_vma=False,
    )
```

```python
import math

import jax
import jax.numpy as jnp
from jax import lax
from jax.experimental import pallas as pl
from jax.experimental.pallas import tpu as pltpu
from jax.sharding import PartitionSpec as P

FREQ = 6144
LAGS = 2048
ROUNDS = 3
BINS = 2
FINE = 32
BF16 = jnp.bfloat16


def shifted(block, axis, distance):
    devices = range(lax.axis_size(axis))
    route = [((i - distance) % len(devices), i) for i in devices]
    return lax.ppermute(block, axis, route)


def contract_last(a, b, out_type=jnp.float32):
    return lax.dot_general(a, b, (((1,), (1,)), ((), ())), preferred_element_type=out_type)


def pick_rows(planes, index):
    ids = jnp.arange(planes.shape[0], dtype=jnp.int32)
    hot = (index[:, None] == ids[None, :]).astype(BF16)
    return lax.dot_general(hot, planes, (((1,), (0,)), ((), ())), preferred_element_type=BF16)


def parts_of(rows):
    rows = rows.astype(jnp.float32)
    if rows.ndim == 3:
        return rows[:, 0], rows[:, 1]
    half = rows.shape[1] // 2
    return rows[:, :half], rows[:, half:]


def cross_spectra(first, second):
    ar, ai = parts_of(first)
    br, bi = parts_of(second)
    return jnp.concatenate([ar * br + ai * bi, ai * br - ar * bi], axis=1).astype(BF16)


def make_table(freq_index):
    def small(taus):
        phase = jnp.mod(taus[:, None] * freq_index[None, :], 2 * FREQ)
        angle = phase.astype(jnp.float32) * (math.pi / FREQ)
        return jnp.cos(angle), jnp.sin(angle)

    coarse = small(jnp.arange(LAGS // FINE, dtype=jnp.int32) * FINE - LAGS // 2)
    fine = small(jnp.arange(FINE, dtype=jnp.int32))
    (ca, sa), (cb, sb) = lax.optimization_barrier((coarse, fine))
    ca, sa, cb, sb = ca[:, None], sa[:, None], cb[None], sb[None]
    cos = (ca * cb - sa * sb).astype(BF16).reshape(LAGS, -1)
    neg_sin = (-(sa * cb + ca * sb)).astype(BF16).reshape(LAGS, -1)
    return jnp.concatenate([cos, neg_sin], axis=1)


def exchanged(axes, distance, block):
    route = [(i, i ^ distance) for i in range(math.prod(lax.axis_size(a) for a in axes))]
    return lax.ppermute(block, axes, route)


def summed(terms):
    total = terms[0].astype(jnp.float32)
    for term in terms[1:]:
        total = total + term.astype(jnp.float32)
    return total.astype(BF16)


def stack_kernel(rows_ref, corr_ref, out_ref):
    chans, bins, _ = out_ref.shape
    first = pl.program_id(0) * chans
    ids = first + lax.broadcasted_iota(jnp.int32, (chans, 1), 0)
    for k in range(bins):
        hot = jnp.where(ids * bins + k == rows_ref[...], 1.0, 0.0).astype(BF16)
        out_ref[:, k, :] = contract_last(hot, corr_ref[...])


def stack_rows(rows, corr, block_chans):
    lags, count = corr.shape
    tile = 128
    return pl.pallas_call(
        stack_kernel,
        grid=(pl.cdiv(block_chans, tile),),
        out_shape=jax.ShapeDtypeStruct((block_chans, BINS, lags), jnp.float32),
        in_specs=[
            pl.BlockSpec((1, count), lambda i: (0, 0)),
            pl.BlockSpec((lags, count), lambda i: (0, 0)),
        ],
        out_specs=pl.BlockSpec((tile, BINS, lags), lambda i: (i, 0, 0)),
        compiler_params=pltpu.CompilerParams(vmem_limit_bytes=40 * 2**20),
        cost_estimate=pl.CostEstimate(
            flops=2 * block_chans * BINS * lags * count,
            bytes_accessed=4 * block_chans * BINS * lags + 2 * lags * count,
            transcendentals=0,
        ),
    )(rows[None, :], corr)


def per_device(spectra, pair_local, pair_partner, pair_bin, pair_owner, pair_count):
    blocks = lax.axis_size("chan")
    segs, halves = lax.axis_size("seg"), lax.axis_size("lag")
    me = lax.axis_index("chan")
    lag_index = lax.axis_index("lag")
    seg_index = lax.axis_index("seg")
    own = spectra[0]
    block_chans, _, half_freq = own.shape
    half_lags = LAGS // halves
    share = half_lags // segs
    slots = pair_local.shape[2]
    half = slots // 2
    slot_ids = jnp.arange(slots, dtype=jnp.int32)

    def before(r):
        return lax.rem(me - r + blocks, blocks)

    def leaving(r, lo, hi):
        return pair_partner[before(r), r, 0::2][lo:hi], pair_local[me, r, 1::2][lo:hi]

    def arrive(r, to_first, to_partner):
        return shifted(to_first, "chan", -r), shifted(to_partner, "chan", r)

    def arrive_rows(r):
        to_first, to_partner = leaving(r, 0, half)
        if 2 * r % blocks == 0:
            index = jnp.concatenate([to_first, to_partner])
            rows = shifted(jnp.take(own, index, axis=0), "chan", r)
            return rows[:half], rows[half:]
        return arrive(r, *(jnp.take(own, index, axis=0) for index in (to_first, to_partner)))

    near = arrive_rows(1)
    planes = jnp.concatenate([own[:, 0], own[:, 1]], axis=1)
    far = arrive_rows(2)

    freq_index = lag_index * half_freq + jnp.arange(half_freq, dtype=jnp.int32) + 1
    table = make_table(freq_index)
    corr_scale = FREQ ** (-0.5)

    def correlate(cross):
        return (contract_last(table, cross) * corr_scale).astype(BF16)

    def peers():
        for distance in range(1, halves * segs):
            lag, seg = lag_index ^ (distance % halves), seg_index ^ (distance // halves)
            yield distance, lag, seg

    def reduce_share(part):
        def cut(lag, seg):
            return lax.dynamic_slice_in_dim(part, lag * half_lags + seg * share, share, 0)

        terms = [cut(lag_index, seg_index)]
        for distance, lag, seg in peers():
            terms.append(exchanged(("seg", "lag"), distance, cut(lag, seg)))
        return summed(terms)

    def reduce_in_steps(part):
        def cut(lag):
            return lax.dynamic_slice_in_dim(part, lag * half_lags, half_lags, 0)

        terms = [cut(lag_index)]
        for distance in range(1, halves):
            terms.append(exchanged(("lag",), distance, cut(lag_index ^ distance)))
        part = summed(terms)

        def cut_share(seg):
            return lax.dynamic_slice_in_dim(part, seg * share, share, 0)

        terms = [cut_share(seg_index)]
        for distance in range(1, segs):
            terms.append(exchanged(("seg",), distance, cut_share(seg_index ^ distance)))
        return summed(terms)

    def gather_shares(shares):
        whole = jnp.zeros((half_lags, shares.shape[1]), BF16)
        for distance in range(segs):
            block = exchanged(("seg",), distance, shares) if distance else shares
            whole = lax.dynamic_update_slice(whole, block, ((seg_index ^ distance) * share, 0))
        return whole

    def crosses(r, lo, hi, second, first):
        return [
            cross_spectra(pick_rows(planes, pair_local[me, r, 0::2][lo:hi]), second),
            cross_spectra(first, pick_rows(planes, pair_partner[before(r), r, 1::2][lo:hi])),
        ]

    def swapped(r, corr):
        here = corr.shape[1] // 2
        if 2 * r % blocks == 0:
            back = shifted(corr, "chan", r)
            return [corr, back[:, here:], back[:, :here]]
        return [corr, *arrive(r, corr[:, here:], corr[:, :here])]

    def target(channel, b, r, owner, pick):
        live = (slot_ids < pair_count[b, r]) & (pair_owner[b, r] == owner)
        return pick(jnp.where(live, channel[b, r] * BINS + pair_bin[b, r], -1))

    def targets(r, lo, hi):
        even, odd = (lambda v: v[0::2][lo:hi]), (lambda v: v[1::2][lo:hi])
        return [
            target(pair_local, me, r, 0, even),
            target(pair_partner, before(r), r, 1, odd),
            target(pair_local, me, r, 0, odd),
            target(pair_partner, before(r), r, 1, even),
        ]

    own_cross = cross_spectra(
        pick_rows(planes, pair_local[me, 0]), pick_rows(planes, pair_partner[me, 0])
    )
    own_rows = jnp.where(pair_owner[me, 0] == 0, pair_local[me, 0], pair_partner[me, 0])
    own_rows = jnp.where(slot_ids < pair_count[me, 0], own_rows * BINS + pair_bin[me, 0], -1)

    near_part = correlate(jnp.concatenate([own_cross, *crosses(1, 0, half, *near)], axis=0))
    near_corr = reduce_in_steps(near_part)
    near_pieces = [near_corr[:, :slots], *swapped(1, near_corr[:, slots:])]
    near_corr = gather_shares(jnp.concatenate(near_pieces, axis=1))
    near_corr, far = lax.optimization_barrier((near_corr, far))
    far_corr = reduce_share(correlate(jnp.concatenate(crosses(2, 0, half, *far), axis=0)))
    far_corr = gather_shares(jnp.concatenate(swapped(2, far_corr), axis=1))

    rows = [own_rows, *targets(1, 0, half), *targets(2, 0, half)]
    corr = jnp.concatenate([near_corr, far_corr], axis=1)
    return stack_rows(jnp.concatenate(rows), corr, block_chans)


def solution(mesh):
    return jax.shard_map(
        per_device,
        mesh=mesh,
        in_specs=(P("seg", "chan", None, "lag"), P(), P(), P(), P(), P()),
        out_specs=P("chan", None, "lag"),
        check_vma=False,
    )
```

```python
import math

import jax
import jax.numpy as jnp
from jax import lax
from jax.experimental import pallas as pl
from jax.experimental.pallas import tpu as pltpu
from jax.sharding import PartitionSpec as P

FREQ = 6144
LAGS = 2048
ROUNDS = 3
BINS = 2
FINE = 32
BF16 = jnp.bfloat16


def shifted(block, axis, distance):
    devices = range(lax.axis_size(axis))
    route = [((i - distance) % len(devices), i) for i in devices]
    return lax.ppermute(block, axis, route)


def contract_last(a, b, out_type=jnp.float32):
    return lax.dot_general(a, b, (((1,), (1,)), ((), ())), preferred_element_type=out_type)


def pick_rows(planes, index):
    ids = jnp.arange(planes.shape[0], dtype=jnp.int32)
    hot = (index[:, None] == ids[None, :]).astype(BF16)
    return lax.dot_general(hot, planes, (((1,), (0,)), ((), ())), preferred_element_type=BF16)


def parts_of(rows):
    rows = rows.astype(jnp.float32)
    if rows.ndim == 3:
        return rows[:, 0], rows[:, 1]
    half = rows.shape[1] // 2
    return rows[:, :half], rows[:, half:]


def cross_spectra(first, second):
    ar, ai = parts_of(first)
    br, bi = parts_of(second)
    return jnp.concatenate([ar * br + ai * bi, ai * br - ar * bi], axis=1).astype(BF16)


def make_table(freq_index):
    def small(taus):
        phase = jnp.mod(taus[:, None] * freq_index[None, :], 2 * FREQ)
        angle = phase.astype(jnp.float32) * (math.pi / FREQ)
        return jnp.cos(angle), jnp.sin(angle)

    coarse = small(jnp.arange(LAGS // FINE, dtype=jnp.int32) * FINE - LAGS // 2)
    fine = small(jnp.arange(FINE, dtype=jnp.int32))
    (ca, sa), (cb, sb) = lax.optimization_barrier((coarse, fine))
    ca, sa, cb, sb = ca[:, None], sa[:, None], cb[None], sb[None]
    cos = (ca * cb - sa * sb).astype(BF16).reshape(LAGS, -1)
    neg_sin = (-(sa * cb + ca * sb)).astype(BF16).reshape(LAGS, -1)
    return jnp.concatenate([cos, neg_sin], axis=1)


def exchanged(axes, distance, block):
    route = [(i, i ^ distance) for i in range(math.prod(lax.axis_size(a) for a in axes))]
    return lax.ppermute(block, axes, route)


def summed(terms):
    total = terms[0].astype(jnp.float32)
    for term in terms[1:]:
        total = total + term.astype(jnp.float32)
    return total.astype(BF16)


def stack_kernel(rows_ref, corr_ref, out_ref):
    chans, bins, _ = out_ref.shape
    first = pl.program_id(0) * chans
    ids = first + lax.broadcasted_iota(jnp.int32, (chans, 1), 0)
    for k in range(bins):
        hot = jnp.where(ids * bins + k == rows_ref[...], 1.0, 0.0).astype(BF16)
        out_ref[:, k, :] = contract_last(hot, corr_ref[...])


def stack_rows(rows, corr, block_chans):
    lags, count = corr.shape
    tile = 128
    return pl.pallas_call(
        stack_kernel,
        grid=(pl.cdiv(block_chans, tile),),
        out_shape=jax.ShapeDtypeStruct((block_chans, BINS, lags), jnp.float32),
        in_specs=[
            pl.BlockSpec((1, count), lambda i: (0, 0)),
            pl.BlockSpec((lags, count), lambda i: (0, 0)),
        ],
        out_specs=pl.BlockSpec((tile, BINS, lags), lambda i: (i, 0, 0)),
        compiler_params=pltpu.CompilerParams(vmem_limit_bytes=40 * 2**20),
        cost_estimate=pl.CostEstimate(
            flops=2 * block_chans * BINS * lags * count,
            bytes_accessed=4 * block_chans * BINS * lags + 2 * lags * count,
            transcendentals=0,
        ),
    )(rows[None, :], corr)


def per_device(spectra, pair_local, pair_partner, pair_bin, pair_owner, pair_count):
    blocks = lax.axis_size("chan")
    segs, halves = lax.axis_size("seg"), lax.axis_size("lag")
    me = lax.axis_index("chan")
    lag_index = lax.axis_index("lag")
    seg_index = lax.axis_index("seg")
    own = spectra[0]
    block_chans, _, half_freq = own.shape
    half_lags = LAGS // halves
    share = half_lags // segs
    slots = pair_local.shape[2]
    half = slots // 2
    slot_ids = jnp.arange(slots, dtype=jnp.int32)

    def before(r):
        return lax.rem(me - r + blocks, blocks)

    def leaving(r, lo, hi):
        return pair_partner[before(r), r, 0::2][lo:hi], pair_local[me, r, 1::2][lo:hi]

    def arrive(r, to_first, to_partner):
        return shifted(to_first, "chan", -r), shifted(to_partner, "chan", r)

    def arrive_rows(r):
        to_first, to_partner = leaving(r, 0, half)
        if 2 * r % blocks == 0:
            index = jnp.concatenate([to_first, to_partner])
            rows = shifted(jnp.take(own, index, axis=0), "chan", r)
            return rows[:half], rows[half:]
        return arrive(r, *(jnp.take(own, index, axis=0) for index in (to_first, to_partner)))

    near = arrive_rows(1)
    planes = jnp.concatenate([own[:, 0], own[:, 1]], axis=1)
    far = arrive_rows(2)

    freq_index = lag_index * half_freq + jnp.arange(half_freq, dtype=jnp.int32) + 1
    table = make_table(freq_index)
    corr_scale = FREQ ** (-0.5)

    def correlate(cross):
        return (contract_last(table, cross) * corr_scale).astype(BF16)

    def peers():
        for distance in range(1, halves * segs):
            lag, seg = lag_index ^ (distance % halves), seg_index ^ (distance // halves)
            yield distance, lag, seg

    def reduce_share(part):
        def cut(lag, seg):
            return lax.dynamic_slice_in_dim(part, lag * half_lags + seg * share, share, 0)

        terms = [cut(lag_index, seg_index)]
        for distance, lag, seg in peers():
            terms.append(exchanged(("seg", "lag"), distance, cut(lag, seg)))
        return summed(terms)

    def reduce_in_steps(part):
        def cut(lag):
            return lax.dynamic_slice_in_dim(part, lag * half_lags, half_lags, 0)

        terms = [cut(lag_index)]
        for distance in range(1, halves):
            terms.append(exchanged(("lag",), distance, cut(lag_index ^ distance)))
        part = summed(terms)

        def cut_share(seg):
            return lax.dynamic_slice_in_dim(part, seg * share, share, 0)

        terms = [cut_share(seg_index)]
        for distance in range(1, segs):
            terms.append(exchanged(("seg",), distance, cut_share(seg_index ^ distance)))
        return summed(terms)

    def gather_shares(shares):
        whole = jnp.zeros((half_lags, shares.shape[1]), BF16)
        for distance in range(segs):
            block = exchanged(("seg",), distance, shares) if distance else shares
            whole = lax.dynamic_update_slice(whole, block, ((seg_index ^ distance) * share, 0))
        return whole

    def crosses(r, lo, hi, second, first):
        return [
            cross_spectra(pick_rows(planes, pair_local[me, r, 0::2][lo:hi]), second),
            cross_spectra(first, pick_rows(planes, pair_partner[before(r), r, 1::2][lo:hi])),
        ]

    def swapped(r, corr):
        here = corr.shape[1] // 2
        if 2 * r % blocks == 0:
            back = shifted(corr, "chan", r)
            return [corr, back[:, here:], back[:, :here]]
        return [corr, *arrive(r, corr[:, here:], corr[:, :here])]

    def target(channel, b, r, owner, pick):
        live = (slot_ids < pair_count[b, r]) & (pair_owner[b, r] == owner)
        return pick(jnp.where(live, channel[b, r] * BINS + pair_bin[b, r], -1))

    def targets(r, lo, hi):
        even, odd = (lambda v: v[0::2][lo:hi]), (lambda v: v[1::2][lo:hi])
        return [
            target(pair_local, me, r, 0, even),
            target(pair_partner, before(r), r, 1, odd),
            target(pair_local, me, r, 0, odd),
            target(pair_partner, before(r), r, 1, even),
        ]

    own_cross = cross_spectra(
        pick_rows(planes, pair_local[me, 0]), pick_rows(planes, pair_partner[me, 0])
    )
    own_rows = jnp.where(pair_owner[me, 0] == 0, pair_local[me, 0], pair_partner[me, 0])
    own_rows = jnp.where(slot_ids < pair_count[me, 0], own_rows * BINS + pair_bin[me, 0], -1)

    own_part, near = lax.optimization_barrier((correlate(own_cross), near))
    near_part = correlate(jnp.concatenate(crosses(1, 0, half, *near), axis=0))
    near_part = jnp.concatenate([own_part, near_part], axis=1)
    near_corr = reduce_in_steps(near_part)
    near_pieces = [near_corr[:, :slots], *swapped(1, near_corr[:, slots:])]
    near_corr = gather_shares(jnp.concatenate(near_pieces, axis=1))
    near_corr, far = lax.optimization_barrier((near_corr, far))
    far_corr = reduce_share(correlate(jnp.concatenate(crosses(2, 0, half, *far), axis=0)))
    far_corr = gather_shares(jnp.concatenate(swapped(2, far_corr), axis=1))

    rows = [own_rows, *targets(1, 0, half), *targets(2, 0, half)]
    corr = jnp.concatenate([near_corr, far_corr], axis=1)
    return stack_rows(jnp.concatenate(rows), corr, block_chans)


def solution(mesh):
    return jax.shard_map(
        per_device,
        mesh=mesh,
        in_specs=(P("seg", "chan", None, "lag"), P(), P(), P(), P(), P()),
        out_specs=P("chan", None, "lag"),
        check_vma=False,
    )
```
